256 devices in a mesh: hi: 8 (over y_lo, x), lo: 32 (over z, y_hi, core).
Axes of the slice: x: 4, y: 4 (y_hi: 2, y_lo: 2; y = y_hi * 2 + y_lo), z: 8, core: 2. Of those that a mesh axis runs over, the one named last changes fastest.
Arguments:
- density: float32 [16, 1048576], P(None, ('hi', 'lo')), may hold values from -6 to 6
- points: float32 [3, 1048576], P(None, ('hi', 'lo')), may hold values from 0 to 1
- leaf_basis: float32 [8192, 64, 128], P(('hi', 'lo')), may hold values from -0.5 to 0.5
- leaf_interp: float32 [8192, 64, 128], P(('hi', 'lo')), may hold values from -0.75 to 0.75
- translate: float32 [8, 8192, 64, 128], P(None, ('hi', 'lo')), may hold values from -0.5 to 0.5
- offsets: int32 [8192, 4], P(('hi', 'lo')), may hold values from -2 to 2, as said below
- counts: int32 [8192], P(('hi', 'lo')), may hold values from 0 to 4, as said below
Outputs:
- potential: float32 [16, 1048576], P(None, ('hi', 'lo'))
The draws below stay inside these ranges and needn't reach their ends.
Inputs may be any that keep to these rules, and one draw needn't show every extreme that they name: The 4 offsets of a leaf are distinct; only the first counts entries of a leaf are used. Over the 32 leaves of one device the counts sum to at most 64, and some device reaches that sum in every draw.
All inputs are finite; a program needn't handle non-finite values.
Results may differ from the reference program's by a relative error of at most 0.0003.
Values sent between devices are 32-bit elements; how exact they have to be, the bound alone decides.
A program may use at most 64 MiB of HBM per device.

```python
import math
import jax
import jax.numpy as jnp
from jax import lax

RHS = 16
LEAF = 128
RANK = 64
NL = 32
REACH = 2
NB_MAX = 4
LEVELS = 8
LEAVES = 8192
N = 1048576
N_HI = 8
N_LO = 32


def draw_offsets(key, part):
    key = jax.random.fold_in(key, 7)
    width_all = 2 * REACH + 1
    scores = jax.random.randint(key, (LEAVES, width_all), 0, 1 << 20) * width_all + jnp.arange(width_all, dtype=jnp.int32)[None, :]
    order = jnp.argsort(scores, axis=1, stable=True).astype(jnp.int32)
    return (order[:, :NB_MAX] - REACH).astype(jnp.int32)


def draw_counts(key, part):
    key = jax.random.fold_in(key, 11)
    key_flag, key_pick, key_first, key_second = jax.random.split(key, 4)
    devices_all = LEAVES // NL
    flags = jax.random.randint(key_flag, (devices_all,), 0, 2)
    chosen = jax.random.randint(key_pick, (), 0, devices_all)
    filled = (flags == 1) | (jnp.arange(devices_all, dtype=jnp.int32) == chosen)
    first = jax.random.randint(key_first, (devices_all, NL // 2), 0, NB_MAX + 1)
    spread = jax.random.randint(key_second, (devices_all, NL // 2), 0, 1 << 20)
    second_free = spread % (NB_MAX - first + 1)
    second = jnp.where(filled[:, None], NB_MAX - first, second_free)
    return jnp.stack([first, second], axis=-1).reshape(LEAVES).astype(jnp.int32)


def level_of(rng, extent, cuts, low, top_value):
    level, own = 1.0, jax.random.fold_in(rng, 6)
    for axis_at, blocks in cuts:
        heights = jnp.exp(jax.random.uniform(jax.random.fold_in(own, axis_at), (blocks,), jnp.float32, low / len(cuts), top_value / len(cuts)))
        level = level * jnp.repeat(heights, extent[axis_at] // blocks).reshape([-1 if axis == axis_at else 1 for axis in range(len(extent))])
    return level


def noise(own_key, dims, width, limit, pieces=(), kind=jnp.bfloat16):
    gain = level_of(own_key, dims, pieces, -0.22, 0.18) if pieces else 1.0
    entries = jax.random.normal(own_key, dims, jnp.float32) * width * gain
    return jnp.minimum(jnp.maximum(entries, -limit), limit).astype(kind)


def setup_inputs(seed: int = 0) -> dict:
    splits = jax.random.split(jax.random.key(seed), 8)
    return {
        "density": noise(splits[0], (RHS, N), 1.0, 6.0, ((1, 256),), jnp.float32),
        "points": jnp.clip(1.0 * jax.random.uniform(splits[1], (3, N), jnp.float32) ** level_of(splits[1], (3, N), ((1, 256),), -0.2, 0.2), 0.0, 1.0),
        "leaf_basis": noise(splits[2], (LEAVES, RANK, LEAF), LEAF ** -0.5, 0.5, ((0, 256),), jnp.float32),
        "leaf_interp": noise(splits[3], (LEAVES, RANK, LEAF), RANK ** -0.5, 0.75, ((0, 256),), jnp.float32),
        "translate": noise(splits[4], (LEVELS, LEAVES, RANK, 2 * RANK), (2 * RANK) ** -0.5, 0.5, ((1, 256),), jnp.float32),
        "offsets": draw_offsets(jax.random.fold_in(splits[7], 71), 0),
        "counts": draw_counts(jax.random.fold_in(splits[7], 71), 0),
    }


HIGH = lax.Precision.HIGHEST
SPACING = 0.5
WAVENUM = 3.0
SOFTEN = 0.1
STRENGTH = 0.0625

def kernel_apply(target_pts, source_set, shift_ids, weights):
    dens_rows = source_set.shape[1] - 3
    half_rows = dens_rows // 2
    along = shift_ids.astype(jnp.float32)[:, None, None] * SPACING
    delta_x = along + source_set[:, dens_rows, None, :] - target_pts[:, 0, :, None]
    delta_y = source_set[:, dens_rows + 1, None, :] - target_pts[:, 1, :, None]
    delta_z = source_set[:, dens_rows + 2, None, :] - target_pts[:, 2, :, None]
    distance = jnp.sqrt(delta_x * delta_x + delta_y * delta_y + delta_z * delta_z + SOFTEN * SOFTEN)
    factor = weights[:, None, None] * STRENGTH / distance
    real_part = jnp.cos(WAVENUM * distance) * factor
    imag_part = jnp.sin(WAVENUM * distance) * factor
    source_dens = source_set[:, :dens_rows]
    turned = jnp.concatenate([-source_dens[:, half_rows:], source_dens[:, :half_rows]], axis=1)
    first = jnp.einsum('nab,nrb->nra', real_part, source_dens, precision=HIGH)
    second = jnp.einsum('nab,nrb->nra', imag_part, turned, precision=HIGH)
    return first + second

def reference(density, points, leaf_basis, leaf_interp, translate, offsets, counts):
    leaf_blocks = density.reshape(RHS, LEAVES, LEAF)
    state = jnp.einsum('rij,ikj->rik', leaf_blocks, leaf_basis, precision=HIGH)
    lo_bits = N_LO.bit_length() - 1
    hi_bits = N_HI.bit_length() - 1
    level_bits = [level_idx % (lo_bits + hi_bits) for level_idx in range(LEVELS)]
    device_ids = jnp.arange(N_HI * N_LO, dtype=jnp.int32)
    leaf_local = jnp.arange(NL, dtype=jnp.int32)
    for level_idx in range(LEVELS):
        partner_dev = jnp.bitwise_xor(device_ids, jnp.int32(1 << level_bits[level_idx]))
        leaf_order = (partner_dev[:, None] * NL + leaf_local[None, :]).reshape(-1)
        partner = jnp.take(state, leaf_order, axis=1)
        level_mats = translate[level_idx]
        state = jnp.einsum('rik,ikm->rim', state, level_mats[:, :, :RANK], precision=HIGH) + jnp.einsum('rik,ikm->rim', partner, level_mats[:, :, RANK:], precision=HIGH)
    far_field = jnp.einsum('rik,ikj->rij', state, leaf_interp, precision=HIGH)
    sources = jnp.concatenate([density, points], axis=0).reshape(RHS + 3, LEAVES, LEAF).transpose(1, 0, 2)
    target_all = points.reshape(3, LEAVES, LEAF).transpose(1, 0, 2)
    group_size = math.gcd(LEAVES, 256)

    def leaf_group(leaf_ids):
        target_pts = jnp.take(target_all, leaf_ids, axis=0)
        used = jnp.take(counts, leaf_ids)
        accum = jnp.zeros((group_size, RHS, LEAF), jnp.float32)
        for slot_idx in range(NB_MAX):
            shift_ids = jnp.take(offsets[:, slot_idx], leaf_ids)
            weights = (used > slot_idx).astype(jnp.float32)
            source_ids = jnp.mod(leaf_ids + shift_ids, LEAVES).astype(jnp.int32)
            source_set = jnp.take(sources, source_ids, axis=0)
            accum = accum + kernel_apply(target_pts, source_set, shift_ids, weights)
        return accum
    near_field = lax.map(leaf_group, jnp.arange(LEAVES, dtype=jnp.int32).reshape(-1, group_size))
    near_field = near_field.reshape(LEAVES, RHS, LEAF).transpose(1, 0, 2)
    return (far_field + near_field).reshape(RHS, N)
```

```python
import functools

import jax
import jax.numpy as jnp
import numpy as np
from jax import lax
from jax.experimental import pallas as pl
from jax.experimental.pallas import tpu as pltpu
from jax.sharding import PartitionSpec as P

MESH = pl.DeviceIdType.MESH
F32 = jnp.float32
BF16 = jnp.bfloat16
SPACING = 0.5
WAVENUM = 3.0
SOFTEN = 0.1
STRENGTH = 0.0625
RHS = 16
LEAF = 128
RANK = 64
PAD = 2
CHUNKS = 4


def fit(func, degree, low, high):
    mid, half = (low + high) / 2, (high - low) / 2
    cheb = np.polynomial.chebyshev.Chebyshev.interpolate(lambda v: func(v * half + mid), degree)
    poly = cheb.convert(kind=np.polynomial.Polynomial).coef
    return [float(c / half**k) for k, c in enumerate(poly)]


T_LOW, T_HIGH = SOFTEN**2 * 0.99, (2 * SPACING + 1) ** 2 + 2 + SOFTEN**2
T_MID = (T_LOW + T_HIGH) / 2
HALF_K = WAVENUM / 2
COS_COEF = fit(lambda t: np.cos(HALF_K * np.sqrt(t)) * np.sqrt(2 * STRENGTH), 6, T_LOW, T_HIGH)
SIN_COEF = fit(lambda t: np.sin(HALF_K * np.sqrt(t)) / np.sqrt(t) * np.sqrt(2 * STRENGTH), 5, T_LOW, T_HIGH)


def horner(coefs, u):
    acc = u * coefs[-1] + coefs[-2]
    for c in coefs[-3::-1]:
        acc = acc * u + c
    return acc


def split2(x):
    hi = x.astype(BF16)
    lo = (x - hi.astype(F32)).astype(BF16)
    return hi, lo


def split3(x):
    a = x.astype(BF16).astype(F32)
    rest = x - a
    b = rest.astype(BF16).astype(F32)
    return a, b, rest - b


def lane_low(shape):
    return lax.broadcasted_iota(jnp.int32, shape, 1) < RANK


def fold(r, rows):
    return r[:rows, :128] + r[:rows, 128:] + r[rows:, :128]


def wide(w):
    hi, lo = split2(w)
    return jnp.concatenate([hi, lo], axis=1)


def tall(x):
    hi, lo = split2(x)
    return jnp.concatenate([hi, lo], axis=0)


def coef_pair(d0, d1, basis):
    x = tall(jnp.concatenate([d0, d1], axis=0))
    r = lax.dot_general(x, tall(basis), (((1,), (1,)), ((), ())), preferred_element_type=F32)
    a = fold(r, 2 * RHS)
    return jnp.where(lane_low((RHS, 128)), a[:RHS], a[RHS:])


def level_pair(own, part, mats):
    x = jnp.concatenate([own, part], axis=0)
    low = lane_low((2 * RHS, 128))
    zero = jnp.zeros_like(x)
    x = tall(jnp.concatenate([jnp.where(low, x, zero), jnp.where(low, zero, x)], axis=0))
    a = fold(jnp.dot(x, wide(mats), preferred_element_type=F32), 4 * RHS)
    own0, part0, own1, part1 = (a[i * RHS : (i + 1) * RHS] for i in range(4))
    low = lane_low((RHS, 128))
    return jnp.where(low, own0, part1) + pltpu.roll(jnp.where(low, own1, part0), RANK, 1)


def interp_pair(state, mats):
    low = lane_low((RHS, 128))
    zero = jnp.zeros_like(state)
    x = tall(jnp.concatenate([jnp.where(low, state, zero), jnp.where(low, zero, state)], axis=0))
    return fold(jnp.dot(x, wide(mats), preferred_element_type=F32), 2 * RHS)


def rows8(*rows):
    index = lax.broadcasted_iota(jnp.int32, (8, LEAF), 0)
    out = jnp.zeros((8, LEAF), F32)
    for i, row in enumerate(rows):
        out = jnp.where(index == i, jnp.broadcast_to(row, (8, LEAF)) if not isinstance(row, float) else row, out)
    return out


def kernel(
    n_hi, n_lo, leaves,
    dens_h, pts_h, basis_h, interp_h, trans_h, off_h, cnt_h, out_ref,
    dens, pts, basis, interp, trans, off, cnt, nxt, halo_d, halo_p, own, part, feat, coords, srcs, items,
    in_sem, basis_sem, trans_sem, send_sem, recv_sem, halo_send, halo_recv,
):
    levels, pairs = trans.shape[0], trans.shape[1]
    per = pairs // CHUNKS
    slots = off.shape[0]
    hi, lo = lax.axis_index("hi"), lax.axis_index("lo")
    flat = hi * n_lo + lo
    total = n_hi * n_lo

    def place(index):
        return (index // n_lo, index % n_lo)

    def partner(bit):
        return place(flat + bit * (1 - 2 * ((flat // bit) % 2)))

    right = place((flat + 1) % total)
    left = place((flat + total - 1) % total)

    barrier = pltpu.get_barrier_semaphore()
    for level in range(levels):
        pl.semaphore_signal(barrier, inc=1, device_id=partner(1 << level), device_id_type=MESH)
    for side in (left, right):
        pl.semaphore_signal(barrier, inc=1, device_id=side, device_id_type=MESH)

    load_dens = pltpu.make_async_copy(dens_h, dens, in_sem.at[0])
    load_pts = pltpu.make_async_copy(pts_h, pts, in_sem.at[1])
    load_off = pltpu.make_async_copy(off_h, off, in_sem.at[2])
    load_cnt = pltpu.make_async_copy(cnt_h, cnt, in_sem.at[3])
    load_interp = pltpu.make_async_copy(interp_h, interp, in_sem.at[4])
    load_basis = [
        pltpu.make_async_copy(basis_h.at[pl.ds(c * per, per)], basis.at[pl.ds(c * per, per)], basis_sem.at[c])
        for c in range(CHUNKS)
    ]

    def load_trans(level):
        return pltpu.make_async_copy(trans_h.at[level], trans.at[level], trans_sem.at[level])

    load_dens.start()
    for copy in load_basis:
        copy.start()
    load_trans(0).start()
    load_pts.start()
    load_off.start()
    load_cnt.start()
    for level in range(1, levels):
        load_trans(level).start()
    load_interp.start()

    def send(level, chunk, target):
        return pltpu.make_async_remote_copy(
            src_ref=own.at[level, pl.ds(chunk * per, per)],
            dst_ref=part.at[level, pl.ds(chunk * per, per)],
            send_sem=send_sem.at[level, chunk],
            recv_sem=recv_sem.at[level, chunk],
            device_id=target,
            device_id_type=MESH,
        )

    halo_copies = []
    edge = (leaves - PAD) * LEAF
    for i, (start, side, target) in enumerate(((edge, 0, right), (0, 1, left))):
        for j, (src, dst) in enumerate(((dens, halo_d), (pts, halo_p))):
            halo_copies.append(
                pltpu.make_async_remote_copy(
                    src_ref=src.at[:, pl.ds(start, PAD * LEAF)],
                    dst_ref=dst.at[side],
                    send_sem=halo_send.at[2 * i + j],
                    recv_sem=halo_recv.at[2 * i + j],
                    device_id=target,
                    device_id_type=MESH,
                )
            )

    load_dens.wait()
    for c in range(CHUNKS):
        load_basis[c].wait()

        def coef_step(i, _, c=c):
            p = c * per + i
            base = pl.multiple_of(p * 2 * LEAF, 2 * LEAF)
            block = dens[:, pl.ds(base, 2 * LEAF)]
            own[0, p] = coef_pair(block[:, :LEAF], block[:, LEAF:], basis[p])
            return 0

        lax.fori_loop(0, per, coef_step, 0, unroll=True)
    load_pts.wait()
    pl.semaphore_wait(barrier, levels + 2)
    for c in range(CHUNKS):
        send(0, c, partner(1)).start()
    for copy in halo_copies:
        copy.start()

    def level_task(level, chunk):
        for i in range(per):
            p = chunk * per + i
            own[level + 1, p] = level_pair(own[level, p], part[level, p], trans[level, p])

    load_trans(0).wait()

    def first_task(chunk, _):
        send(0, chunk, partner(1)).wait()
        level_task(0, chunk)
        send(1, chunk, partner(2)).start()
        return 0

    lax.fori_loop(0, CHUNKS, first_task, 0)

    def prepare(e, d, p):
        turned = jnp.concatenate([-d[RHS // 2 :], d[: RHS // 2]], axis=0)
        srcs[e] = tall(jnp.concatenate([d, turned], axis=1))
        x, y, z = (p[k : k + 1] - 0.5 for k in range(3))
        rows = rows8(x, y, z, x * x + y * y + z * z, 1.0)
        coords[e] = rows
        a, b, c = split3(rows)
        feat[e] = jnp.concatenate([a, a, b, b, a, c], axis=0).T.astype(BF16)

    def prepare_own(q, _):
        base = pl.multiple_of(q * LEAF, LEAF)
        prepare(q + PAD, dens[:, pl.ds(base, LEAF)], pts[:, pl.ds(base, LEAF)])
        return 0

    lax.fori_loop(0, leaves, prepare_own, 0, unroll=2)
    load_off.wait()
    load_cnt.wait()

    def link_step(i, following):
        q = leaves - 1 - i
        nxt[q + 1] = following
        return jnp.where(cnt[q] > 0, q, following)

    first_leaf = lax.fori_loop(0, leaves, link_step, jnp.int32(leaves - 1))
    for copy in halo_copies:
        copy.wait()
    for side in range(2):
        for i in range(PAD):
            e = side * (leaves + PAD) + i
            prepare(e, halo_d[side, :, i * LEAF : (i + 1) * LEAF], halo_p[side, :, i * LEAF : (i + 1) * LEAF])

    def item(j, leaf, slot, acc):
        shift = off[jnp.minimum(slot, slots - 1), leaf]
        source = leaf + shift + PAD
        p = coords[leaf + PAD]
        x = p[0:1] - SPACING * shift.astype(F32)
        y, z = p[1:2], p[2:3]
        rows = rows8(-2 * x, -2 * y, -2 * z, 1.0, x * x + y * y + z * z + SOFTEN * SOFTEN)
        a, b, c = split3(rows)
        target = jnp.concatenate([a, b, a, b, c, a], axis=0).astype(BF16)
        t = jnp.dot(feat[source], target, preferred_element_type=F32)
        u = t - T_MID
        cosine = horner(COS_COEF, u)
        real = (cosine * cosine - STRENGTH) * lax.rsqrt(t)
        imag = horner(SIN_COEF, u) * cosine
        mats = jnp.concatenate([wide(real), wide(imag)], axis=0)
        r = fold(jnp.dot(srcs[source], mats, preferred_element_type=F32), RHS)
        acc = r + jnp.where(slot == 0, 0.0, acc)
        items[j] = acc
        slot = slot + 1
        done = slot >= cnt[leaf]
        return jnp.where(done, nxt[leaf + 1], leaf), jnp.where(done, 0, slot), acc

    def unit(k, carry):
        leaf, slot, acc = carry
        for i in range(2):
            leaf, slot, acc = item(2 * k + i, leaf, slot, acc)
        return leaf, slot, acc

    units = items.shape[0] // 2
    every = units // ((levels - 1) * CHUNKS)
    spare = units - every * (levels - 1) * CHUNKS
    carry = (first_leaf, jnp.int32(0), jnp.zeros((RHS, LEAF), F32))
    carry = lax.fori_loop(0, spare, unit, carry)

    def middle_level(level, state):
        bit, carry = state
        load_trans(level).wait()

        def task(chunk, carry):
            start = spare + ((level - 1) * CHUNKS + chunk) * every
            carry = lax.fori_loop(start, start + every, unit, carry)
            send(level, chunk, partner(bit)).wait()
            level_task(level, chunk)
            send(level + 1, chunk, partner(bit * 2)).start()
            return carry

        return bit * 2, lax.fori_loop(0, CHUNKS, task, carry)

    bit, carry = lax.fori_loop(1, levels - 1, middle_level, (jnp.int32(2), carry))
    last = levels - 1
    for chunk in range(CHUNKS):
        start = spare + ((last - 1) * CHUNKS + chunk) * every
        carry = lax.fori_loop(start, start + every, unit, carry)
    load_trans(last).wait()
    load_interp.wait()

    def last_task(chunk, end):
        send(last, chunk, partner(1 << last)).wait()
        level_task(last, chunk)
        for i in range(per):
            p = chunk * per + i
            far = interp_pair(own[levels, p], interp[p])
            for h in range(2):
                q = 2 * p + h
                count = cnt[q]
                end = end + count
                near = jnp.where(count > 0, items[jnp.maximum(end - 1, 0)], 0.0)
                out_ref[:, pl.ds(pl.multiple_of(q * LEAF, LEAF), LEAF)] = far[h * RHS : (h + 1) * RHS] + near
        return end

    lax.fori_loop(0, CHUNKS, last_task, jnp.int32(0))


def solution(mesh):
    n_hi, n_lo = mesh.shape["hi"], mesh.shape["lo"]

    def shards(density, points, leaf_basis, leaf_interp, translate, offsets, counts):
        leaves = leaf_basis.shape[0]
        levels = translate.shape[0]
        pairs = leaves // 2
        ext = leaves + 2 * PAD
        capacity = leaves * offsets.shape[1] // 2
        any_spec = pl.BlockSpec(memory_space=pl.ANY)
        dma = pltpu.SemaphoreType.DMA
        return pl.pallas_call(
            functools.partial(kernel, n_hi, n_lo, leaves),
            out_shape=jax.ShapeDtypeStruct(density.shape, F32),
            in_specs=[any_spec] * 7,
            out_specs=pl.BlockSpec(memory_space=pltpu.VMEM),
            scratch_shapes=[
                pltpu.VMEM(density.shape, F32),
                pltpu.VMEM(points.shape, F32),
                pltpu.VMEM((pairs, 128, 128), F32),
                pltpu.VMEM((pairs, 128, 128), F32),
                pltpu.VMEM((levels, pairs, 128, 128), F32),
                pltpu.SMEM(offsets.shape[::-1], jnp.int32),
                pltpu.SMEM(counts.shape, jnp.int32),
                pltpu.SMEM((leaves + 1,), jnp.int32),
                pltpu.VMEM((2, RHS, PAD * LEAF), F32),
                pltpu.VMEM((2, 3, PAD * LEAF), F32),
                pltpu.VMEM((levels + 1, pairs, RHS, 128), F32),
                pltpu.VMEM((levels, pairs, RHS, 128), F32),
                pltpu.VMEM((ext, LEAF, 48), BF16),
                pltpu.VMEM((ext, 8, LEAF), F32),
                pltpu.VMEM((ext, 2 * RHS, 2 * LEAF), BF16),
                pltpu.VMEM((capacity, RHS, LEAF), F32),
                dma((5,)),
                dma((CHUNKS,)),
                dma((levels,)),
                dma((levels, CHUNKS)),
                dma((levels, CHUNKS)),
                dma((4,)),
                dma((4,)),
            ],
            compiler_params=pltpu.CompilerParams(
                collective_id=0, has_side_effects=True, vmem_limit_bytes=60 << 20
            ),
            name="helmholtz",
        )(
            density,
            points,
            leaf_basis.reshape(pairs, 2 * RANK, LEAF),
            leaf_interp.reshape(pairs, 2 * RANK, LEAF),
            translate.reshape(levels, pairs, 2 * RANK, 2 * RANK),
            offsets.T,
            counts,
        )

    return jax.shard_map(
        shards,
        mesh=mesh,
        in_specs=(
            P(None, ("hi", "lo")),
            P(None, ("hi", "lo")),
            P(("hi", "lo"), None, None),
            P(("hi", "lo"), None, None),
            P(None, ("hi", "lo"), None, None),
            P(("hi", "lo"), None),
            P(("hi", "lo")),
        ),
        out_specs=P(None, ("hi", "lo")),
        check_vma=False,
    )
```

```python
import functools

import jax
import jax.numpy as jnp
import numpy as np
from jax import lax
from jax.experimental import pallas as pl
from jax.experimental.pallas import tpu as pltpu
from jax.sharding import PartitionSpec as P

MESH = pl.DeviceIdType.MESH
F32 = jnp.float32
BF16 = jnp.bfloat16
SPACING = 0.5
WAVENUM = 3.0
SOFTEN = 0.1
STRENGTH = 0.0625
RHS = 16
LEAF = 128
RANK = 64
PAD = 2
CHUNKS = 4
FIRST = (1, 3, 3, 4, 3, 3, 3)
SECOND = (3, 4, 4, 4, 2, 2, 1)


def fit(func, degree, low, high):
    mid, half = (low + high) / 2, (high - low) / 2
    cheb = np.polynomial.chebyshev.Chebyshev.interpolate(lambda v: func(v * half + mid), degree)
    poly = cheb.convert(kind=np.polynomial.Polynomial).coef
    return [float(c / half**k) for k, c in enumerate(poly)]


T_LOW, T_HIGH = SOFTEN**2 * 0.99, (2 * SPACING + 1) ** 2 + 2 + SOFTEN**2
T_MID = (T_LOW + T_HIGH) / 2
HALF_K = WAVENUM / 2
COS_COEF = fit(lambda t: np.cos(HALF_K * np.sqrt(t)) * np.sqrt(2 * STRENGTH), 6, T_LOW, T_HIGH)
SIN_COEF = fit(lambda t: np.sin(HALF_K * np.sqrt(t)) / np.sqrt(t) * np.sqrt(2 * STRENGTH), 5, T_LOW, T_HIGH)


def horner(coefs, u):
    acc = u * coefs[-1] + coefs[-2]
    for c in coefs[-3::-1]:
        acc = acc * u + c
    return acc


def split2(x):
    hi = x.astype(BF16)
    lo = (x - hi.astype(F32)).astype(BF16)
    return hi, lo


def split3(x):
    a = x.astype(BF16).astype(F32)
    rest = x - a
    b = rest.astype(BF16).astype(F32)
    return a, b, rest - b


def lane_low(shape):
    return lax.broadcasted_iota(jnp.int32, shape, 1) < RANK


def fold(r, rows):
    return r[:rows, :128] + r[:rows, 128:] + r[rows:, :128]


def wide(w):
    hi, lo = split2(w)
    return jnp.concatenate([hi, lo], axis=1)


def tall(x):
    hi, lo = split2(x)
    return jnp.concatenate([hi, lo], axis=0)


def coef_pair(d0, d1, basis):
    x = tall(jnp.concatenate([d0, d1], axis=0))
    r = lax.dot_general(x, tall(basis), (((1,), (1,)), ((), ())), preferred_element_type=F32)
    a = fold(r, 2 * RHS)
    return jnp.where(lane_low((RHS, 128)), a[:RHS], a[RHS:])


def level_pair(own, part, mats):
    hi, lo = split2(jnp.concatenate([own, part], axis=0))
    x = jnp.concatenate(
        [jnp.concatenate([hi, hi], axis=1), jnp.concatenate([lo, jnp.zeros_like(lo)], axis=1)], axis=0
    )
    zero = jnp.zeros((RANK, 128), BF16)

    def diagonal(m):
        top = jnp.concatenate([m[:RANK], zero], axis=0)
        return jnp.concatenate([top, jnp.concatenate([zero, m[RANK:]], axis=0)], axis=1)

    weights = jnp.concatenate([diagonal(m) for m in split2(mats)], axis=0)
    r = jnp.dot(x, weights, preferred_element_type=F32)
    a = r[: 2 * RHS] + r[2 * RHS :]
    low = lane_low((RHS, 128))
    kept = jnp.where(low, a[:RHS, :128], a[RHS:, 128:])
    return kept + pltpu.roll(jnp.where(low, a[:RHS, 128:], a[RHS:, :128]), RANK, 1)


def interp_pair(state, mats):
    low = lane_low((RHS, 128))
    zero = jnp.zeros_like(state)
    x = tall(jnp.concatenate([jnp.where(low, state, zero), jnp.where(low, zero, state)], axis=0))
    return fold(jnp.dot(x, wide(mats), preferred_element_type=F32), 2 * RHS)


def rows8(*rows):
    index = lax.broadcasted_iota(jnp.int32, (8, LEAF), 0)
    out = jnp.zeros((8, LEAF), F32)
    for i, row in enumerate(rows):
        out = jnp.where(index == i, jnp.broadcast_to(row, (8, LEAF)) if not isinstance(row, float) else row, out)
    return out


def kernel(
    n_hi, n_lo, leaves,
    dens_h, pts_h, basis_h, interp_h, trans_h, off_h, cnt_h, out_h, near_h,
    dens, pts, basis, interp, trans, off, cnt, nxt, halo_d, halo_p, own, part, feat, coords, srcs, items, out_ref, near_ref,
    in_sem, basis_sem, trans_sem, send_sem, recv_sem, halo_send, halo_recv, out_sem, near_sem,
):
    levels, pairs = trans.shape[0], trans.shape[1]
    per = pairs // CHUNKS
    slots = off.shape[0]
    hi, lo = lax.axis_index("hi"), lax.axis_index("lo")
    flat = hi * n_lo + lo
    total = n_hi * n_lo

    def place(index):
        return (index // n_lo, index % n_lo)

    def partner(bit):
        return place(flat + bit * (1 - 2 * ((flat // bit) % 2)))

    right = place((flat + 1) % total)
    left = place((flat + total - 1) % total)

    barrier = pltpu.get_barrier_semaphore()
    for level in range(levels):
        pl.semaphore_signal(barrier, inc=1, device_id=partner(1 << level), device_id_type=MESH)
    for side in (left, right):
        pl.semaphore_signal(barrier, inc=1, device_id=side, device_id_type=MESH)

    load_dens = pltpu.make_async_copy(dens_h, dens, in_sem.at[0])
    load_pts = pltpu.make_async_copy(pts_h, pts, in_sem.at[1])
    load_off = pltpu.make_async_copy(off_h, off, in_sem.at[2])
    load_cnt = pltpu.make_async_copy(cnt_h, cnt, in_sem.at[3])
    load_interp = pltpu.make_async_copy(interp_h, interp, in_sem.at[4])
    load_basis = [
        pltpu.make_async_copy(basis_h.at[pl.ds(c * per, per)], basis.at[pl.ds(c * per, per)], basis_sem.at[c])
        for c in range(CHUNKS)
    ]

    def load_trans(level):
        return pltpu.make_async_copy(trans_h.at[level], trans.at[level], trans_sem.at[level])

    load_dens.start()
    for copy in load_basis:
        copy.start()
    load_pts.start()

    def send(level, chunk, target):
        return pltpu.make_async_remote_copy(
            src_ref=own.at[level, pl.ds(chunk * per, per)],
            dst_ref=part.at[level, pl.ds(chunk * per, per)],
            send_sem=send_sem.at[level, chunk],
            recv_sem=recv_sem.at[level, chunk],
            device_id=target,
            device_id_type=MESH,
        )

    halo_copies = []
    edge = (leaves - PAD) * LEAF
    for i, (start, side, target) in enumerate(((edge, 0, right), (0, 1, left))):
        for j, (src, dst) in enumerate(((dens, halo_d), (pts, halo_p))):
            halo_copies.append(
                pltpu.make_async_remote_copy(
                    src_ref=src.at[:, pl.ds(start, PAD * LEAF)],
                    dst_ref=dst.at[side],
                    send_sem=halo_send.at[2 * i + j],
                    recv_sem=halo_recv.at[2 * i + j],
                    device_id=target,
                    device_id_type=MESH,
                )
            )

    load_dens.wait()
    for c in range(CHUNKS):
        load_basis[c].wait()

        def coef_step(i, _, c=c):
            p = c * per + i
            base = pl.multiple_of(p * 2 * LEAF, 2 * LEAF)
            block = dens[:, pl.ds(base, 2 * LEAF)]
            own[0, p] = coef_pair(block[:, :LEAF], block[:, LEAF:], basis[p])
            return 0

        lax.fori_loop(0, per, coef_step, 0, unroll=True)
        if c == 0:
            pl.semaphore_wait(barrier, levels + 2)
        send(0, c, partner(1)).start()
    load_off.start()
    load_cnt.start()
    for level in range(levels):
        load_trans(level).start()
    load_interp.start()
    load_pts.wait()
    for copy in halo_copies:
        copy.start()

    def level_task(level, chunk):
        places = [chunk * per + i for i in range(per)]
        return [level_pair(own[level, p], part[level, p], trans[level, p]) for p in places]

    load_trans(0).wait()

    def first_task(chunk, _):
        send(0, chunk, partner(1)).wait()
        for i, out in enumerate(level_task(0, chunk)):
            own[1, chunk * per + i] = out
        send(1, chunk, partner(2)).start()
        return 0

    lax.fori_loop(0, CHUNKS, first_task, 0)

    def prepare(e, d, p):
        turned = jnp.concatenate([-d[RHS // 2 :], d[: RHS // 2]], axis=0)
        srcs[e] = tall(jnp.concatenate([d, turned], axis=1))
        x, y, z = (p[k : k + 1] - 0.5 for k in range(3))
        rows = rows8(x, y, z, x * x + y * y + z * z, 1.0)
        coords[e] = rows
        a, b, c = split3(rows)
        feat[e] = jnp.concatenate([a, a, b, b, a, c], axis=0).T.astype(BF16)

    def prepare_own(q, _):
        base = pl.multiple_of(q * LEAF, LEAF)
        prepare(q + PAD, dens[:, pl.ds(base, LEAF)], pts[:, pl.ds(base, LEAF)])
        return 0

    lax.fori_loop(0, leaves, prepare_own, 0, unroll=2)
    load_off.wait()
    load_cnt.wait()

    def link_step(i, following):
        q = leaves - 1 - i
        nxt[q + 1] = following
        return jnp.where(cnt[q] > 0, q, following)

    first_leaf = lax.fori_loop(0, leaves, link_step, jnp.int32(leaves - 1))
    for copy in halo_copies:
        copy.wait()
    for side in range(2):
        for i in range(PAD):
            e = side * (leaves + PAD) + i
            prepare(e, halo_d[side, :, i * LEAF : (i + 1) * LEAF], halo_p[side, :, i * LEAF : (i + 1) * LEAF])

    def item(j, leaf, slot, acc):
        shift = off[jnp.minimum(slot, slots - 1), leaf]
        source = leaf + shift + PAD
        p = coords[leaf + PAD]
        x = p[0:1] - SPACING * shift.astype(F32)
        y, z = p[1:2], p[2:3]
        rows = rows8(-2 * x, -2 * y, -2 * z, 1.0, x * x + y * y + z * z + SOFTEN * SOFTEN)
        a, b, c = split3(rows)
        target = jnp.concatenate([a, b, a, b, c, a], axis=0).astype(BF16)
        t = jnp.dot(feat[source], target, preferred_element_type=F32)
        u = t - T_MID
        cosine = horner(COS_COEF, u)
        real = (cosine * cosine - STRENGTH) * lax.rsqrt(t)
        imag = horner(SIN_COEF, u) * cosine
        mats = jnp.concatenate([wide(real), wide(imag)], axis=0)
        r = fold(jnp.dot(srcs[source], mats, preferred_element_type=F32), RHS)
        acc = r + jnp.where(slot == 0, 0.0, acc)
        items[j] = acc
        slot = slot + 1
        done = slot >= cnt[leaf]
        return jnp.where(done, nxt[leaf + 1], leaf), jnp.where(done, 0, slot), acc

    total_items = items.shape[0]
    last = levels - 1

    def fill(level, chunk, state):
        n = jnp.int32(0)
        for i, (first, second) in enumerate(zip(FIRST, SECOND)):
            n = jnp.where(level == i + 1, jnp.where(lo % 2 == 0, first, second), n)
        n = jnp.where(chunk == 0, n, 0)

        def body(_, state):
            return one(one(state))

        return lax.fori_loop(0, n, body, state)

    def one(state):
        k, leaf, slot, acc = state
        return (k + 1, *item(k, leaf, slot, acc))

    def middle_level(level, state):
        bit, state = state
        load_trans(level).wait()

        def task(chunk, state):
            state = fill(level, chunk, state)
            send(level, chunk, partner(bit)).wait()
            outs = level_task(level, chunk)
            state = one(state)
            for i, out in enumerate(outs):
                own[level + 1, chunk * per + i] = out
            send(level + 1, chunk, partner(bit * 2)).start()
            return state

        return bit * 2, lax.fori_loop(0, CHUNKS, task, state)

    state = (jnp.int32(0), first_leaf, jnp.int32(0), jnp.zeros((RHS, LEAF), F32))
    bit, state = lax.fori_loop(1, last, middle_level, (jnp.int32(2), state))
    done = [CHUNKS * (levels - 2) + 2 * sum(t[: levels - 2]) for t in (FIRST, SECOND)]
    rest = jnp.where(lo % 2 == 0, *[(total_items - d) // 2 for d in done])
    lax.fori_loop(0, rest, lambda _, state: one(one(state)), state)
    def gather(q, end):
        count = cnt[q]
        end = end + count
        near = jnp.where(count > 0, items[jnp.maximum(end - 1, 0)], 0.0)
        near_ref[:, pl.ds(pl.multiple_of(q * LEAF, LEAF), LEAF)] = near
        return end

    lax.fori_loop(0, leaves, gather, jnp.int32(0), unroll=4)
    store_near = pltpu.make_async_copy(near_ref, near_h, near_sem.at[0])
    store_near.start()
    load_trans(last).wait()
    load_interp.wait()

    def store_out(chunk):
        columns = pl.ds(chunk * per * 2 * LEAF, per * 2 * LEAF)
        if not isinstance(chunk, int):
            columns = pl.ds(pl.multiple_of(chunk * per * 2 * LEAF, LEAF), per * 2 * LEAF)
        return pltpu.make_async_copy(out_ref.at[:, columns], out_h.at[:, columns], out_sem.at[chunk])

    def last_task(chunk, _):
        send(last, chunk, partner(1 << last)).wait()
        outs = level_task(last, chunk)
        for i in range(per):
            p = chunk * per + i
            far = interp_pair(outs[i], interp[p])
            for h in range(2):
                base = pl.multiple_of((2 * p + h) * LEAF, LEAF)
                out_ref[:, pl.ds(base, LEAF)] = far[h * RHS : (h + 1) * RHS]
        store_out(chunk).start()
        return 0

    lax.fori_loop(0, CHUNKS, last_task, 0)
    store_near.wait()
    for chunk in range(CHUNKS):
        store_out(chunk).wait()


def solution(mesh):
    n_hi, n_lo = mesh.shape["hi"], mesh.shape["lo"]

    def shards(density, points, leaf_basis, leaf_interp, translate, offsets, counts):
        leaves = leaf_basis.shape[0]
        levels = translate.shape[0]
        pairs = leaves // 2
        ext = leaves + 2 * PAD
        capacity = leaves * offsets.shape[1] // 2
        any_spec = pl.BlockSpec(memory_space=pl.ANY)
        dma = pltpu.SemaphoreType.DMA
        far, near = pl.pallas_call(
            functools.partial(kernel, n_hi, n_lo, leaves),
            out_shape=[jax.ShapeDtypeStruct(density.shape, F32)] * 2,
            in_specs=[any_spec] * 7,
            out_specs=[any_spec] * 2,
            scratch_shapes=[
                pltpu.VMEM(density.shape, F32),
                pltpu.VMEM(points.shape, F32),
                pltpu.VMEM((pairs, 128, 128), F32),
                pltpu.VMEM((pairs, 128, 128), F32),
                pltpu.VMEM((levels, pairs, 128, 128), F32),
                pltpu.SMEM(offsets.shape[::-1], jnp.int32),
                pltpu.SMEM(counts.shape, jnp.int32),
                pltpu.SMEM((leaves + 1,), jnp.int32),
                pltpu.VMEM((2, RHS, PAD * LEAF), F32),
                pltpu.VMEM((2, 3, PAD * LEAF), F32),
                pltpu.VMEM((levels, pairs, RHS, 128), F32),
                pltpu.VMEM((levels, pairs, RHS, 128), F32),
                pltpu.VMEM((ext, LEAF, 48), BF16),
                pltpu.VMEM((ext, 8, LEAF), F32),
                pltpu.VMEM((ext, 2 * RHS, 2 * LEAF), BF16),
                pltpu.VMEM((capacity, RHS, LEAF), F32),
                pltpu.VMEM(density.shape, F32),
                pltpu.VMEM(density.shape, F32),
                dma((5,)),
                dma((CHUNKS,)),
                dma((levels,)),
                dma((levels, CHUNKS)),
                dma((levels, CHUNKS)),
                dma((4,)),
                dma((4,)),
                dma((CHUNKS,)),
                dma((1,)),
            ],
            compiler_params=pltpu.CompilerParams(
                collective_id=0, has_side_effects=True, vmem_limit_bytes=60 << 20
            ),
            name="helmholtz",
        )(
            density,
            points,
            leaf_basis.reshape(pairs, 2 * RANK, LEAF),
            leaf_interp.reshape(pairs, 2 * RANK, LEAF),
            translate.reshape(levels, pairs, 2 * RANK, 2 * RANK),
            offsets.T,
            counts,
        )
        return far + near

    return jax.shard_map(
        shards,
        mesh=mesh,
        in_specs=(
            P(None, ("hi", "lo")),
            P(None, ("hi", "lo")),
            P(("hi", "lo"), None, None),
            P(("hi", "lo"), None, None),
            P(None, ("hi", "lo"), None, None),
            P(("hi", "lo"), None),
            P(("hi", "lo")),
        ),
        out_specs=P(None, ("hi", "lo")),
        check_vma=False,
    )
```

```python
import functools

import jax
import jax.numpy as jnp
import numpy as np
from jax import lax
from jax.experimental import pallas as pl
from jax.experimental.pallas import tpu as pltpu
from jax.sharding import PartitionSpec as P

MESH = pl.DeviceIdType.MESH
F32 = jnp.float32
BF16 = jnp.bfloat16
SPACING = 0.5
WAVENUM = 3.0
SOFTEN = 0.1
STRENGTH = 0.0625
RHS = 16
LEAF = 128
RANK = 64
PAD = 2
CHUNKS = 4
FIRST = (1, 3, 3, 4, 3, 3, 3)
SECOND = (5, 5, 5, 4, 1, 0, 0)


def fit(func, degree, low, high):
    mid, half = (low + high) / 2, (high - low) / 2
    cheb = np.polynomial.chebyshev.Chebyshev.interpolate(lambda v: func(v * half + mid), degree)
    poly = cheb.convert(kind=np.polynomial.Polynomial).coef
    return [float(c / half**k) for k, c in enumerate(poly)]


T_LOW, T_HIGH = SOFTEN**2 * 0.99, (2 * SPACING + 1) ** 2 + 2 + SOFTEN**2
T_MID = (T_LOW + T_HIGH) / 2
HALF_K = WAVENUM / 2
COS_COEF = fit(lambda t: np.cos(HALF_K * np.sqrt(t)) * np.sqrt(2 * STRENGTH), 6, T_LOW, T_HIGH)
SIN_COEF = fit(lambda t: np.sin(HALF_K * np.sqrt(t)) / np.sqrt(t) * np.sqrt(2 * STRENGTH), 5, T_LOW, T_HIGH)


def horner(coefs, u):
    acc = u * coefs[-1] + coefs[-2]
    for c in coefs[-3::-1]:
        acc = acc * u + c
    return acc


def split2(x):
    hi = x.astype(BF16)
    lo = (x - hi.astype(F32)).astype(BF16)
    return hi, lo


def split3(x):
    a = x.astype(BF16).astype(F32)
    rest = x - a
    b = rest.astype(BF16).astype(F32)
    return a, b, rest - b


def lane_low(shape):
    return lax.broadcasted_iota(jnp.int32, shape, 1) < RANK


def fold(r, rows):
    return r[:rows, :128] + r[:rows, 128:] + r[rows:, :128]


def wide(w):
    hi, lo = split2(w)
    return jnp.concatenate([hi, lo], axis=1)


def tall(x):
    hi, lo = split2(x)
    return jnp.concatenate([hi, lo], axis=0)


def coef_pair(d0, d1, basis):
    x = tall(jnp.concatenate([d0, d1], axis=0))
    r = lax.dot_general(x, tall(basis), (((1,), (1,)), ((), ())), preferred_element_type=F32)
    a = fold(r, 2 * RHS)
    return jnp.where(lane_low((RHS, 128)), a[:RHS], a[RHS:])


def level_pair(own, part, mats):
    hi, lo = split2(jnp.concatenate([own, part], axis=0))
    x = jnp.concatenate(
        [jnp.concatenate([hi, hi], axis=1), jnp.concatenate([lo, jnp.zeros_like(lo)], axis=1)], axis=0
    )
    zero = jnp.zeros((RANK, 128), BF16)

    def diagonal(m):
        top = jnp.concatenate([m[:RANK], zero], axis=0)
        return jnp.concatenate([top, jnp.concatenate([zero, m[RANK:]], axis=0)], axis=1)

    weights = jnp.concatenate([diagonal(m) for m in split2(mats)], axis=0)
    r = jnp.dot(x, weights, preferred_element_type=F32)
    a = r[: 2 * RHS] + r[2 * RHS :]
    low = lane_low((RHS, 128))
    kept = jnp.where(low, a[:RHS, :128], a[RHS:, 128:])
    return kept + pltpu.roll(jnp.where(low, a[:RHS, 128:], a[RHS:, :128]), RANK, 1)


def interp_pair(state, mats):
    low = lane_low((RHS, 128))
    zero = jnp.zeros_like(state)
    x = tall(jnp.concatenate([jnp.where(low, state, zero), jnp.where(low, zero, state)], axis=0))
    return fold(jnp.dot(x, wide(mats), preferred_element_type=F32), 2 * RHS)


def rows8(*rows):
    index = lax.broadcasted_iota(jnp.int32, (8, LEAF), 0)
    out = jnp.zeros((8, LEAF), F32)
    for i, row in enumerate(rows):
        out = jnp.where(index == i, jnp.broadcast_to(row, (8, LEAF)) if not isinstance(row, float) else row, out)
    return out


def kernel(
    n_hi, n_lo, leaves,
    dens_h, pts_h, basis_h, interp_h, trans_h, off_h, cnt_h, out_h, near_h,
    dens, pts, basis, interp, trans, off, cnt, nxt, halo_d, halo_p, own, part, feat, coords, srcs, items, out_ref, near_ref,
    in_sem, basis_sem, trans_sem, send_sem, recv_sem, halo_send, halo_recv, out_sem, near_sem,
):
    levels, pairs = trans.shape[0], trans.shape[1]
    per = pairs // CHUNKS
    slots = off.shape[0]
    hi, lo = lax.axis_index("hi"), lax.axis_index("lo")
    flat = hi * n_lo + lo
    total = n_hi * n_lo

    def place(index):
        return (index // n_lo, index % n_lo)

    def partner(bit):
        return place(flat + bit * (1 - 2 * ((flat // bit) % 2)))

    right = place((flat + 1) % total)
    left = place((flat + total - 1) % total)

    barrier = pltpu.get_barrier_semaphore()
    for level in range(levels):
        pl.semaphore_signal(barrier, inc=1, device_id=partner(1 << level), device_id_type=MESH)
    for side in (left, right):
        pl.semaphore_signal(barrier, inc=1, device_id=side, device_id_type=MESH)

    load_dens = pltpu.make_async_copy(dens_h, dens, in_sem.at[0])
    load_pts = pltpu.make_async_copy(pts_h, pts, in_sem.at[1])
    load_off = pltpu.make_async_copy(off_h, off, in_sem.at[2])
    load_cnt = pltpu.make_async_copy(cnt_h, cnt, in_sem.at[3])
    load_interp = pltpu.make_async_copy(interp_h, interp, in_sem.at[4])
    load_basis = [
        pltpu.make_async_copy(basis_h.at[pl.ds(c * per, per)], basis.at[pl.ds(c * per, per)], basis_sem.at[c])
        for c in range(CHUNKS)
    ]

    def load_trans(level):
        return pltpu.make_async_copy(trans_h.at[level], trans.at[level], trans_sem.at[level])

    load_dens.start()
    for copy in load_basis:
        copy.start()
    load_pts.start()

    def send(level, chunk, target):
        return pltpu.make_async_remote_copy(
            src_ref=own.at[level, pl.ds(chunk * per, per)],
            dst_ref=part.at[level, pl.ds(chunk * per, per)],
            send_sem=send_sem.at[level, chunk],
            recv_sem=recv_sem.at[level, chunk],
            device_id=target,
            device_id_type=MESH,
        )

    halo_copies = []
    edge = (leaves - PAD) * LEAF
    for i, (start, side, target) in enumerate(((edge, 0, right), (0, 1, left))):
        for j, (src, dst) in enumerate(((dens, halo_d), (pts, halo_p))):
            halo_copies.append(
                pltpu.make_async_remote_copy(
                    src_ref=src.at[:, pl.ds(start, PAD * LEAF)],
                    dst_ref=dst.at[side],
                    send_sem=halo_send.at[2 * i + j],
                    recv_sem=halo_recv.at[2 * i + j],
                    device_id=target,
                    device_id_type=MESH,
                )
            )

    load_dens.wait()
    for c in range(CHUNKS):
        load_basis[c].wait()

        def coef_step(i, _, c=c):
            p = c * per + i
            base = pl.multiple_of(p * 2 * LEAF, 2 * LEAF)
            block = dens[:, pl.ds(base, 2 * LEAF)]
            own[0, p] = coef_pair(block[:, :LEAF], block[:, LEAF:], basis[p])
            return 0

        lax.fori_loop(0, per, coef_step, 0, unroll=True)
        if c == 0:
            pl.semaphore_wait(barrier, levels + 2)
        send(0, c, partner(1)).start()
    load_off.start()
    load_cnt.start()
    for level in range(levels):
        load_trans(level).start()
    load_interp.start()
    load_pts.wait()
    for copy in halo_copies:
        copy.start()

    def level_task(level, chunk):
        places = [chunk * per + i for i in range(per)]
        return [level_pair(own[level, p], part[level, p], trans[level, p]) for p in places]

    load_trans(0).wait()

    def first_task(chunk, _):
        send(0, chunk, partner(1)).wait()
        for i, out in enumerate(level_task(0, chunk)):
            own[1, chunk * per + i] = out
        send(1, chunk, partner(2)).start()
        return 0

    lax.fori_loop(0, CHUNKS, first_task, 0)

    def prepare(e, d, p):
        turned = jnp.concatenate([-d[RHS // 2 :], d[: RHS // 2]], axis=0)
        srcs[e] = tall(jnp.concatenate([d, turned], axis=1))
        x, y, z = (p[k : k + 1] - 0.5 for k in range(3))
        rows = rows8(x, y, z, x * x + y * y + z * z, 1.0)
        coords[e] = rows
        a, b, c = split3(rows)
        feat[e] = jnp.concatenate([a, a, b, b, a, c], axis=0).T.astype(BF16)

    def prepare_own(q, _):
        base = pl.multiple_of(q * LEAF, LEAF)
        prepare(q + PAD, dens[:, pl.ds(base, LEAF)], pts[:, pl.ds(base, LEAF)])
        return 0

    lax.fori_loop(0, leaves, prepare_own, 0, unroll=2)
    load_off.wait()
    load_cnt.wait()

    def link_step(i, following):
        q = leaves - 1 - i
        nxt[q + 1] = following
        return jnp.where(cnt[q] > 0, q, following)

    first_leaf = lax.fori_loop(0, leaves, link_step, jnp.int32(leaves - 1))
    for copy in halo_copies:
        copy.wait()
    for side in range(2):
        for i in range(PAD):
            e = side * (leaves + PAD) + i
            prepare(e, halo_d[side, :, i * LEAF : (i + 1) * LEAF], halo_p[side, :, i * LEAF : (i + 1) * LEAF])

    def item(j, leaf, slot, acc):
        shift = off[jnp.minimum(slot, slots - 1), leaf]
        source = leaf + shift + PAD
        p = coords[leaf + PAD]
        x = p[0:1] - SPACING * shift.astype(F32)
        y, z = p[1:2], p[2:3]
        rows = rows8(-2 * x, -2 * y, -2 * z, 1.0, x * x + y * y + z * z + SOFTEN * SOFTEN)
        a, b, c = split3(rows)
        target = jnp.concatenate([a, b, a, b, c, a], axis=0).astype(BF16)
        t = jnp.dot(feat[source], target, preferred_element_type=F32)
        u = t - T_MID
        cosine = horner(COS_COEF, u)
        real = (cosine * cosine - STRENGTH) * lax.rsqrt(t)
        imag = horner(SIN_COEF, u) * cosine
        mats = jnp.concatenate([wide(real), wide(imag)], axis=0)
        r = fold(jnp.dot(srcs[source], mats, preferred_element_type=F32), RHS)
        acc = r + jnp.where(slot == 0, 0.0, acc)
        items[j] = acc
        slot = slot + 1
        done = slot >= cnt[leaf]
        return jnp.where(done, nxt[leaf + 1], leaf), jnp.where(done, 0, slot), acc

    total_items = items.shape[0]
    last = levels - 1

    def fill(level, chunk, state):
        n = jnp.int32(0)
        for i, (first, second) in enumerate(zip(FIRST, SECOND)):
            n = jnp.where(level == i + 1, jnp.where(lo % 2 == 0, first, second), n)
        n = jnp.where(chunk == 0, n, 0)

        def body(_, state):
            return one(one(state))

        return lax.fori_loop(0, n, body, state)

    def one(state):
        k, leaf, slot, acc = state
        return (k + 1, *item(k, leaf, slot, acc))

    def middle_level(level, state):
        bit, state = state
        load_trans(level).wait()

        def task(chunk, state):
            state = fill(level, chunk, state)
            send(level, chunk, partner(bit)).wait()
            outs = level_task(level, chunk)
            state = one(state)
            for i, out in enumerate(outs):
                own[level + 1, chunk * per + i] = out
            send(level + 1, chunk, partner(bit * 2)).start()
            return state

        return bit * 2, lax.fori_loop(0, CHUNKS, task, state)

    state = (jnp.int32(0), first_leaf, jnp.int32(0), jnp.zeros((RHS, LEAF), F32))
    bit, state = lax.fori_loop(1, last, middle_level, (jnp.int32(2), state))
    done = [CHUNKS * (levels - 2) + 2 * sum(t[: levels - 2]) for t in (FIRST, SECOND)]
    rest = jnp.where(lo % 2 == 0, *[(total_items - d) // 2 for d in done])
    lax.fori_loop(0, rest, lambda _, state: one(one(state)), state)
    def gather(q, end):
        count = cnt[q]
        end = end + count
        near = jnp.where(count > 0, items[jnp.maximum(end - 1, 0)], 0.0)
        near_ref[:, pl.ds(pl.multiple_of(q * LEAF, LEAF), LEAF)] = near
        return end

    lax.fori_loop(0, leaves, gather, jnp.int32(0), unroll=4)
    store_near = pltpu.make_async_copy(near_ref, near_h, near_sem.at[0])
    store_near.start()
    load_trans(last).wait()
    load_interp.wait()

    def store_out(chunk):
        columns = pl.ds(chunk * per * 2 * LEAF, per * 2 * LEAF)
        if not isinstance(chunk, int):
            columns = pl.ds(pl.multiple_of(chunk * per * 2 * LEAF, LEAF), per * 2 * LEAF)
        return pltpu.make_async_copy(out_ref.at[:, columns], out_h.at[:, columns], out_sem.at[chunk])

    def last_task(chunk, _):
        send(last, chunk, partner(1 << last)).wait()
        outs = level_task(last, chunk)
        for i in range(per):
            p = chunk * per + i
            far = interp_pair(outs[i], interp[p])
            for h in range(2):
                base = pl.multiple_of((2 * p + h) * LEAF, LEAF)
                out_ref[:, pl.ds(base, LEAF)] = far[h * RHS : (h + 1) * RHS]
        store_out(chunk).start()
        return 0

    lax.fori_loop(0, CHUNKS, last_task, 0)
    store_near.wait()
    for chunk in range(CHUNKS):
        store_out(chunk).wait()


def solution(mesh):
    n_hi, n_lo = mesh.shape["hi"], mesh.shape["lo"]

    def shards(density, points, leaf_basis, leaf_interp, translate, offsets, counts):
        leaves = leaf_basis.shape[0]
        levels = translate.shape[0]
        pairs = leaves // 2
        ext = leaves + 2 * PAD
        capacity = leaves * offsets.shape[1] // 2
        any_spec = pl.BlockSpec(memory_space=pl.ANY)
        dma = pltpu.SemaphoreType.DMA
        far, near = pl.pallas_call(
            functools.partial(kernel, n_hi, n_lo, leaves),
            out_shape=[jax.ShapeDtypeStruct(density.shape, F32)] * 2,
            in_specs=[any_spec] * 7,
            out_specs=[any_spec] * 2,
            scratch_shapes=[
                pltpu.VMEM(density.shape, F32),
                pltpu.VMEM(points.shape, F32),
                pltpu.VMEM((pairs, 128, 128), F32),
                pltpu.VMEM((pairs, 128, 128), F32),
                pltpu.VMEM((levels, pairs, 128, 128), F32),
                pltpu.SMEM(offsets.shape[::-1], jnp.int32),
                pltpu.SMEM(counts.shape, jnp.int32),
                pltpu.SMEM((leaves + 1,), jnp.int32),
                pltpu.VMEM((2, RHS, PAD * LEAF), F32),
                pltpu.VMEM((2, 3, PAD * LEAF), F32),
                pltpu.VMEM((levels, pairs, RHS, 128), F32),
                pltpu.VMEM((levels, pairs, RHS, 128), F32),
                pltpu.VMEM((ext, LEAF, 48), BF16),
                pltpu.VMEM((ext, 8, LEAF), F32),
                pltpu.VMEM((ext, 2 * RHS, 2 * LEAF), BF16),
                pltpu.VMEM((capacity, RHS, LEAF), F32),
                pltpu.VMEM(density.shape, F32),
                pltpu.VMEM(density.shape, F32),
                dma((5,)),
                dma((CHUNKS,)),
                dma((levels,)),
                dma((levels, CHUNKS)),
                dma((levels, CHUNKS)),
                dma((4,)),
                dma((4,)),
                dma((CHUNKS,)),
                dma((1,)),
            ],
            compiler_params=pltpu.CompilerParams(
                collective_id=0, has_side_effects=True, vmem_limit_bytes=60 << 20
            ),
            name="helmholtz",
        )(
            density,
            points,
            leaf_basis.reshape(pairs, 2 * RANK, LEAF),
            leaf_interp.reshape(pairs, 2 * RANK, LEAF),
            translate.reshape(levels, pairs, 2 * RANK, 2 * RANK),
            offsets.T,
            counts,
        )
        return far + near

    return jax.shard_map(
        shards,
        mesh=mesh,
        in_specs=(
            P(None, ("hi", "lo")),
            P(None, ("hi", "lo")),
            P(("hi", "lo"), None, None),
            P(("hi", "lo"), None, None),
            P(None, ("hi", "lo"), None, None),
            P(("hi", "lo"), None),
            P(("hi", "lo")),
        ),
        out_specs=P(None, ("hi", "lo")),
        check_vma=False,
    )
```
